32 devices in a mesh: band: 4 (over y, x), tm: 8 (over z, core).
Axes of the slice: x: 2, y: 2, z: 4, core: 2. Of those that a mesh axis runs over, the one named last changes fastest.
Arguments:
- chebyshev: float32 [32, 3, 32768], P(None, None, ('band', 'tm')), may hold values from -0.9 to 0.9
- crossing: int32 [4, 2, 512], P('band'), may hold values from 0 to 4095, as said below
- counts: int32 [4], P('band'), may hold values from 4096 to 8192, as said below
- route: int32 [4, 32], P('band'), may hold values from 0 to 31, each once within a row
- pairs: int32 [4, 2, 32], P('band'), may hold values from 0 to 31, each once within a row
Outputs:
- closest: float32 [128, 256, 256], P('band', 'tm')
The draws below stay inside these ranges and needn't reach their ends.
Inputs may be any that keep to these rules, and one draw needn't show every extreme that they name: `crossing`: the 1024 slots of one band are distinct and below 4096, so every band's live slots include them. `counts`: some band is full in every draw. `route`: each row is a permutation of the band's 32 tiles. `pairs`: each row of one owner is a permutation of its 32 received tiles.
All inputs are finite; a program needn't handle non-finite values.
Results may differ from the reference program's by a relative error of at most 0.0003.
Values sent between devices are 32-bit elements; how exact they have to be, the bound alone decides.
A program may use at most 64 MiB of HBM per device.

```python
import jax
import jax.numpy as jnp
from jax import lax

NCOEF = 32
SAMPLES = 64
TILE = 256
TILES_DEV = 32
MIG = 512
BANDS = 4
OBJ_DEV = 8192
OBJECTS = 32768
TILES_PEER = 8
BLOCKS = 128


def draw_crossing(key, part):
    band_keys = jax.random.split(jax.random.fold_in(key, 5), BANDS)

    def one_band(band_key):
        return jax.random.permutation(band_key, OBJ_DEV // 2)[:2 * MIG].reshape(2, MIG)
    return jax.vmap(one_band)(band_keys).astype(jnp.int32)


def draw_counts(key, part):
    key_values = jax.random.fold_in(key, 11)
    key_full = jax.random.fold_in(key, 12)
    values = jax.random.randint(key_values, (BANDS,), OBJ_DEV // 2, OBJ_DEV + 1)
    full_band = jax.random.randint(key_full, (), 0, BANDS)
    return jnp.where(jnp.arange(BANDS) == full_band, OBJ_DEV, values).astype(jnp.int32)


def shard_levels(stream_key, extent, cuts, least, top_value):
    gain = 1.0
    for axis_at, parts in cuts:
        steps = jax.random.uniform(jax.random.fold_in(jax.random.fold_in(stream_key, 6), axis_at), (parts,), jnp.float32, least / len(cuts), top_value / len(cuts))
        gain = gain * jnp.repeat(jnp.exp(steps), extent[axis_at] // parts).reshape((-1,) + (1,) * (len(extent) - 1 - axis_at))
    return gain


def scatter_about(rng, extent, width, most, cuts=(), kind=jnp.bfloat16):
    factor_of = shard_levels(rng, extent, cuts, -0.22, 0.18) if cuts else 1.0
    drawn = jax.random.normal(rng, extent, jnp.float32) * width * factor_of
    return jnp.minimum(jnp.maximum(drawn, -most), most).astype(kind)


def setup_inputs(seed: int = 0) -> dict:
    arg_keys = jax.random.split(jax.random.key(seed), 6)
    chebyshev = scatter_about(arg_keys[0], (NCOEF, 3, OBJECTS), 0.15, 0.9, ((2, 32),), jnp.float32)
    crossing = draw_crossing(jax.random.fold_in(arg_keys[5], 71), 0)
    counts = draw_counts(jax.random.fold_in(arg_keys[5], 71), 0)
    route = jax.vmap(lambda own: jax.random.permutation(own, TILES_DEV))(jax.random.split(arg_keys[3], BANDS)).reshape((BANDS, TILES_DEV)).astype(jnp.int32)
    pairs = jax.vmap(lambda own: jax.random.permutation(own, TILES_DEV))(jax.random.split(arg_keys[4], BANDS * 2)).reshape((BANDS, 2, TILES_DEV)).astype(jnp.int32)
    return {"chebyshev": chebyshev, "crossing": crossing, "counts": counts, "route": route, "pairs": pairs}


def cheb_table():
    sample_times = -1.0 + (2.0 * jnp.arange(SAMPLES, dtype=jnp.float32) + 1.0) / SAMPLES
    orders = jnp.arange(NCOEF, dtype=jnp.float32)
    return jnp.cos(orders[None, :] * jnp.arccos(sample_times)[:, None])


def pick_slots(block_data, index_list):
    return block_data[:, :, index_list]


def place_slots(block_data, rise_ids, fall_ids, below, above):
    return block_data.at[:, :, rise_ids].set(below).at[:, :, fall_ids].set(above)


def closest_gap(first_tile, second_tile):
    diff_x = first_tile[:, 0, :, None] - second_tile[:, 0, None, :]
    diff_y = first_tile[:, 1, :, None] - second_tile[:, 1, None, :]
    diff_z = first_tile[:, 2, :, None] - second_tile[:, 2, None, :]
    return jnp.min((diff_x * diff_x + diff_y * diff_y) + diff_z * diff_z, axis=0)


def reference(chebyshev, crossing, counts, route, pairs):
    per_band = chebyshev.reshape(NCOEF, 3, BANDS, OBJ_DEV).transpose(2, 0, 1, 3)
    rising_ids = crossing[:, 0, :]
    falling_ids = crossing[:, 1, :]
    leave_up = jax.vmap(pick_slots)(per_band, rising_ids)
    leave_down = jax.vmap(pick_slots)(per_band, falling_ids)
    zero_band = jnp.zeros_like(leave_up[:1])
    from_below = jnp.concatenate([zero_band, leave_up[:-1]], axis=0)
    from_above = jnp.concatenate([leave_down[1:], zero_band], axis=0)
    updated = jax.vmap(place_slots)(per_band, rising_ids, falling_ids, from_below, from_above)
    table = cheb_table()
    positions = jnp.einsum("sk,bkco->bsco", table, updated, precision=lax.Precision.HIGHEST)
    alive = (jnp.arange(OBJ_DEV, dtype=jnp.int32)[None, :] < counts[:, None]).astype(jnp.float32)
    pos_tiles = positions.reshape(BANDS, SAMPLES, 3, TILES_DEV, TILE)
    alive_tiles = alive.reshape(BANDS, TILES_DEV, TILE)

    def locate(owner, slot):
        source = slot // TILES_PEER
        return source, route[source, owner * TILES_PEER + slot % TILES_PEER]

    def one_block(block_id):
        owner = block_id // TILES_DEV
        pair_slot = block_id % TILES_DEV
        band_a, tile_a = locate(owner, pairs[owner, 0, pair_slot])
        band_b, tile_b = locate(owner, pairs[owner, 1, pair_slot])
        first_tile = pos_tiles[band_a, :, :, tile_a, :]
        second_tile = pos_tiles[band_b, :, :, tile_b, :]
        pair_mask = alive_tiles[band_a, tile_a][:, None] * alive_tiles[band_b, tile_b][None, :]
        return closest_gap(first_tile, second_tile) * pair_mask

    return lax.map(one_block, jnp.arange(BLOCKS, dtype=jnp.int32))
```

```python
import functools

import jax
import jax.numpy as jnp
import numpy as np
from jax import lax
from jax.experimental import pallas as pl
from jax.experimental.pallas import tpu as pltpu
from jax.sharding import PartitionSpec as P

SAMPLES = 64
HIGHEST = lax.Precision.HIGHEST


def shifted(block, axis, distance):
    devices = range(lax.axis_size(axis))
    route = [(i - distance, i) for i in devices if i - distance in devices]
    return lax.ppermute(block, axis, route)


def basis_table(order_count):
    times = -1.0 + (2.0 * np.arange(SAMPLES) + 1.0) / SAMPLES
    return np.cos(np.arange(order_count)[None, :] * np.arccos(times)[:, None])


def split3(values):
    high = values.astype(jnp.bfloat16)
    rest = values - high.astype(jnp.float32)
    middle = rest.astype(jnp.bfloat16)
    low = (rest - middle.astype(jnp.float32)).astype(jnp.bfloat16)
    return high, middle, low


def join3(product, rows):
    return (product[:rows] + product[rows : 2 * rows]) + product[2 * rows :]


def pick_kernel(slots_ref, shards_ref, rise_ref, fall_ref):
    steps, rows, width = shards_ref.shape
    ranks = slots_ref.shape[0]
    slot_ids = lax.broadcasted_iota(jnp.int32, (ranks, width), 1)
    total = None
    for step in range(steps):
        hit = slots_ref[...] - step * width == slot_ids
        one_hot = hit.astype(jnp.float32).astype(jnp.bfloat16)
        parts = jnp.concatenate(split3(shards_ref[step]), axis=0)
        product = lax.dot_general(
            parts, one_hot, (((1,), (1,)), ((), ())), preferred_element_type=jnp.float32
        )
        total = product if total is None else total + product
    joined = join3(total, rows)
    rise_ref[...] = joined[:, : ranks // 2]
    fall_ref[...] = joined[:, ranks // 2 :]


def pick(whole, slots_column, steps):
    _, rows, width = whole.shape
    ranks = slots_column.shape[0]
    half = jax.ShapeDtypeStruct((rows, ranks // 2), jnp.float32)
    return pl.pallas_call(
        pick_kernel,
        grid=(1,),
        in_specs=[
            pl.BlockSpec((ranks, 1), lambda i: (0, 0)),
            pl.BlockSpec((steps, rows, width), lambda i: (0, 0, 0)),
        ],
        out_specs=[pl.BlockSpec((rows, ranks // 2), lambda i: (0, 0))] * 2,
        out_shape=[half, half],
        compiler_params=pltpu.CompilerParams(vmem_limit_bytes=40 * 2**20),
        name="pick",
    )(slots_column, whole)


def place_kernel(crossing_tiles, route_ref, slots_ref, tile_ref, rise_ref, fall_ref, out_ref, parts):
    step = pl.program_id(0)
    rows, width = tile_ref.shape[1:]
    ranks = slots_ref.shape[0]
    tile_id = route_ref[step]

    @pl.when(step == 0)
    def _():
        joined = jnp.concatenate([rise_ref[...], fall_ref[...]], axis=1)
        parts[...] = jnp.concatenate(split3(joined), axis=0)

    @pl.when(tile_id >= crossing_tiles)
    def _():
        out_ref[...] = tile_ref[...]

    @pl.when(tile_id < crossing_tiles)
    def _():
        slot_ids = lax.broadcasted_iota(jnp.int32, (ranks, width), 1) + tile_id * width
        hit = (slots_ref[...] == slot_ids).astype(jnp.float32)
        one_hot = hit.astype(jnp.bfloat16)
        taken = jnp.sum(hit, axis=0, keepdims=True)
        product = jnp.dot(parts[...], one_hot, preferred_element_type=jnp.float32)
        out_ref[0] = jnp.where(taken > 0.0, join3(product, rows), tile_ref[0])


def place(whole, slots_column, climbers, sinkers, route, tile_size):
    _, rows, width = whole.shape
    ranks = slots_column.shape[0]
    tile_count = route.shape[0]
    per_shard = width // tile_size
    return pl.pallas_call(
        functools.partial(place_kernel, tile_count // 2),
        grid_spec=pltpu.PrefetchScalarGridSpec(
            num_scalar_prefetch=1,
            grid=(tile_count,),
            in_specs=[
                pl.BlockSpec((ranks, 1), lambda i, r: (0, 0)),
                pl.BlockSpec(
                    (1, rows, tile_size),
                    lambda i, r: (r[i] // per_shard, 0, r[i] % per_shard),
                ),
                pl.BlockSpec((rows, ranks // 2), lambda i, r: (0, 0)),
                pl.BlockSpec((rows, ranks // 2), lambda i, r: (0, 0)),
            ],
            out_specs=pl.BlockSpec((1, rows, tile_size), lambda i, r: (i, 0, 0)),
            scratch_shapes=[pltpu.VMEM((3 * rows, ranks), jnp.bfloat16)],
        ),
        out_shape=jax.ShapeDtypeStruct((tile_count, rows, tile_size), jnp.float32),
        compiler_params=pltpu.CompilerParams(vmem_limit_bytes=40 * 2**20),
        name="place",
    )(route, slots_column, whole, climbers, sinkers)


def pair_kernel(
    share,
    first_ids,
    second_ids,
    live,
    place_ref,
    window_ref,
    tile_ref,
    alive_window_ref,
    alive_tile_ref,
    table_ref,
    table_t_ref,
    out_ref,
    turned,
    first_pos,
    second_pos,
):
    step = pl.program_id(0)
    both = live[first_ids[step]] * live[second_ids[step]]

    @pl.when(both == 0)
    def _():
        out_ref[...] = jnp.zeros_like(out_ref)

    @pl.when(both != 0)
    def _():
        window = window_ref[0]
        rows, lanes = window.shape
        flags = jnp.broadcast_to(alive_window_ref[0], (8, lanes))
        turned[...] = jnp.concatenate([window, flags], axis=0).T
        mine = turned[pl.ds(pl.multiple_of(place_ref[1], share), share), :]
        first_pos[...] = jnp.dot(
            mine[:, :rows], table_t_ref[...], precision=HIGHEST, preferred_element_type=jnp.float32
        )
        second_pos[...] = jnp.dot(
            table_ref[...], tile_ref[0], precision=HIGHEST, preferred_element_type=jnp.float32
        )
        closest = None
        for s in range(SAMPLES):
            gaps = [
                first_pos[:, c * SAMPLES + s : c * SAMPLES + s + 1]
                - second_pos[c * SAMPLES + s : c * SAMPLES + s + 1, :]
                for c in range(3)
            ]
            square = (gaps[0] * gaps[0] + gaps[1] * gaps[1]) + gaps[2] * gaps[2]
            closest = square if closest is None else jnp.minimum(closest, square)
        out_ref[0] = closest * (mine[:, rows : rows + 1] * alive_tile_ref[0])


def pair_blocks(tiles, alive, first_ids, second_ids, row_start, share):
    tile_count, rows, tile_size = tiles.shape
    orders = rows // 3
    table = np.kron(np.eye(3), basis_table(orders)).astype(np.float32)
    live = (jnp.max(alive, axis=1) > 0.0).astype(jnp.int32)
    lanes = min(128, tile_size)
    position = jnp.stack([row_start // lanes, row_start % lanes]).astype(jnp.int32)
    alive = alive.reshape(tile_count, 1, tile_size)
    return pl.pallas_call(
        functools.partial(pair_kernel, share),
        grid_spec=pltpu.PrefetchScalarGridSpec(
            num_scalar_prefetch=4,
            grid=(tile_count,),
            in_specs=[
                pl.BlockSpec((1, rows, lanes), lambda i, a, b, l, w: (a[i], 0, w[0])),
                pl.BlockSpec((1, rows, tile_size), lambda i, a, b, l, w: (b[i], 0, 0)),
                pl.BlockSpec((1, 1, lanes), lambda i, a, b, l, w: (a[i], 0, w[0])),
                pl.BlockSpec((1, 1, tile_size), lambda i, a, b, l, w: (b[i], 0, 0)),
                pl.BlockSpec((3 * SAMPLES, rows), lambda i, a, b, l, w: (0, 0)),
                pl.BlockSpec((rows, 3 * SAMPLES), lambda i, a, b, l, w: (0, 0)),
            ],
            out_specs=pl.BlockSpec((1, share, tile_size), lambda i, a, b, l, w: (i, 0, 0)),
            scratch_shapes=[
                pltpu.VMEM((lanes, rows + 8), jnp.float32),
                pltpu.VMEM((share, 3 * SAMPLES), jnp.float32),
                pltpu.VMEM((3 * SAMPLES, tile_size), jnp.float32),
            ],
        ),
        out_shape=jax.ShapeDtypeStruct((tile_count, share, tile_size), jnp.float32),
        compiler_params=pltpu.CompilerParams(vmem_limit_bytes=40 * 2**20),
        name="pair_blocks",
    )(first_ids, second_ids, live, position, tiles, tiles, alive, alive, table, table.T)


def on_device(chebyshev, crossing, counts, route, pairs):
    orders, _, local = chebyshev.shape
    tm_count = lax.axis_size("tm")
    tile_count = route.shape[1]
    obj_count = local * tm_count
    tile_size = obj_count // tile_count
    share = tile_size // tm_count
    row_start = lax.axis_index("tm") * share

    flat = chebyshev.transpose(1, 0, 2).reshape(3 * orders, local)
    whole = lax.all_gather(flat, "tm", axis=0, tiled=False)

    slot_ids = jnp.arange(tile_size, dtype=jnp.int32)[None, :] + tile_size * route[0][:, None]
    alive_out = (slot_ids < counts[0]).astype(jnp.float32)
    alive = lax.all_to_all(alive_out, "band", split_axis=0, concat_axis=0, tiled=True)

    slots_column = crossing[0].reshape(-1, 1)
    rising, falling = pick(whole, slots_column, (tm_count + 1) // 2)
    climbers = shifted(rising, "band", 1)
    sinkers = shifted(falling, "band", -1)
    outgoing = place(whole, slots_column, climbers, sinkers, route[0], tile_size)
    tiles = lax.all_to_all(outgoing, "band", split_axis=0, concat_axis=0, tiled=True)
    return pair_blocks(tiles, alive, pairs[0, 0], pairs[0, 1], row_start, share)


def solution(mesh):
    placed = (
        P(None, None, ("band", "tm")),
        P("band", None, None),
        P("band"),
        P("band", None),
        P("band", None, None),
    )
    return jax.shard_map(
        on_device, mesh=mesh, in_specs=placed, out_specs=P("band", "tm", None), check_vma=False
    )
```

```python
import functools

import jax
import jax.numpy as jnp
import numpy as np
from jax import lax
from jax.experimental import pallas as pl
from jax.experimental.pallas import tpu as pltpu
from jax.sharding import PartitionSpec as P

SAMPLES = 64
HIGHEST = lax.Precision.HIGHEST
MESH = pl.DeviceIdType.MESH


def shifted(block, axis, distance):
    devices = range(lax.axis_size(axis))
    route = [(i - distance, i) for i in devices if i - distance in devices]
    return lax.ppermute(block, axis, route)


def basis_table(order_count):
    times = -1.0 + (2.0 * np.arange(SAMPLES) + 1.0) / SAMPLES
    return np.cos(np.arange(order_count)[None, :] * np.arccos(times)[:, None])


def split3(values):
    high = values.astype(jnp.bfloat16)
    rest = values - high.astype(jnp.float32)
    middle = rest.astype(jnp.bfloat16)
    low = (rest - middle.astype(jnp.float32)).astype(jnp.bfloat16)
    return high, middle, low


def join3(product, rows):
    return (product[:rows] + product[rows : 2 * rows]) + product[2 * rows :]


def greet(devices):
    barrier = pltpu.get_barrier_semaphore()
    for device in devices:
        pl.semaphore_signal(barrier, inc=1, device_id=device, device_id_type=MESH)
    pl.semaphore_wait(barrier, len(devices))


def spread(count, position, core, partner, device_of, source_of, out_ref, sems):
    send, recv, hand, take, own = sems
    local = pltpu.make_async_copy(source_of(position), out_ref.at[position, core], own)
    local.start()
    out = []
    for hop in range(1, count):
        peer = (position + hop) % count
        copy = pltpu.make_async_remote_copy(
            src_ref=source_of(peer),
            dst_ref=out_ref.at[position, core],
            send_sem=send.at[hop],
            recv_sem=recv.at[hop],
            device_id=device_of(peer),
            device_id_type=MESH,
        )
        copy.start()
        out.append(copy)
    handed = []
    for hop in range(count):
        origin = (position + count - hop) % count
        if hop:
            out[hop - 1].wait_recv()
        copy = pltpu.make_async_remote_copy(
            src_ref=source_of(position) if hop == 0 else out_ref.at[origin, core],
            dst_ref=out_ref.at[origin, core],
            send_sem=hand.at[hop],
            recv_sem=take.at[hop],
            device_id=partner,
            device_id_type=MESH,
        )
        copy.start()
        handed.append(copy)
    for copy in handed:
        copy.wait()
    for copy in out:
        copy.wait_send()
    local.wait()


def spread_sems(count):
    return [pltpu.SemaphoreType.DMA((count,))] * 4 + [pltpu.SemaphoreType.DMA]


def gather_kernel(count, flat_ref, out_ref, *sems):
    me = lax.axis_index("tm")
    core = me % 2
    partner = {"tm": me + 1 - 2 * core}
    position = me // 2

    def device_of(peer):
        return {"tm": peer * 2 + core}

    greet([device_of((position + hop) % count) for hop in range(1, count)] + [partner])
    spread(count, position, core, partner, device_of, lambda peer: flat_ref, out_ref, sems)


def gather(flat, tm_count):
    count = tm_count // 2
    out = pl.pallas_call(
        functools.partial(gather_kernel, count),
        in_specs=[pl.BlockSpec(memory_space=pl.ANY)],
        out_specs=pl.BlockSpec(memory_space=pl.ANY),
        out_shape=jax.ShapeDtypeStruct((count, 2) + flat.shape, jnp.float32),
        scratch_shapes=spread_sems(count),
        compiler_params=pltpu.CompilerParams(collective_id=0, has_side_effects=True),
        name="gather",
    )(flat)
    return out.reshape((tm_count,) + flat.shape)


def exchange_kernel(count, tiles_ref, flags_ref, out_ref, flags_out_ref, flag_send, flag_recv, flag_own, *sems):
    me = lax.axis_index("tm")
    core = me % 2
    partner = {"tm": me + 1 - 2 * core}
    position = lax.axis_index("band")

    def device_of(peer):
        return {"band": peer}

    greet([device_of((position + hop) % count) for hop in range(1, count)] + [partner])
    own = pltpu.make_async_copy(flags_ref.at[position], flags_out_ref.at[position], flag_own)
    own.start()
    flags = []
    for hop in range(1, count):
        peer = (position + hop) % count
        copy = pltpu.make_async_remote_copy(
            src_ref=flags_ref.at[peer],
            dst_ref=flags_out_ref.at[position],
            send_sem=flag_send.at[hop],
            recv_sem=flag_recv.at[hop],
            device_id=device_of(peer),
            device_id_type=MESH,
        )
        copy.start()
        flags.append(copy)
    spread(
        count, position, core, partner, device_of, lambda peer: tiles_ref.at[peer], out_ref, sems
    )
    for copy in flags:
        copy.wait()
    own.wait()


def exchange(tiles, flags, band_count):
    half, rows, tile_size = tiles.shape
    each = half // band_count
    tiles = tiles.reshape(band_count, each, rows, tile_size)
    flags = flags.reshape(band_count, 2 * each, tile_size)
    out, flags_out = pl.pallas_call(
        functools.partial(exchange_kernel, band_count),
        in_specs=[pl.BlockSpec(memory_space=pl.ANY)] * 2,
        out_specs=[pl.BlockSpec(memory_space=pl.ANY)] * 2,
        out_shape=[
            jax.ShapeDtypeStruct((band_count, 2, each, rows, tile_size), jnp.float32),
            jax.ShapeDtypeStruct(flags.shape, jnp.float32),
        ],
        scratch_shapes=[
            pltpu.SemaphoreType.DMA((band_count,)),
            pltpu.SemaphoreType.DMA((band_count,)),
            pltpu.SemaphoreType.DMA,
        ]
        + spread_sems(band_count),
        compiler_params=pltpu.CompilerParams(collective_id=1, has_side_effects=True),
        name="exchange",
    )(tiles, flags)
    return out.reshape(2 * half, rows, tile_size), flags_out.reshape(2 * half, tile_size)


def pick_kernel(slots_ref, shards_ref, rise_ref, fall_ref):
    steps, rows, width = shards_ref.shape
    ranks = slots_ref.shape[0]
    slot_ids = lax.broadcasted_iota(jnp.int32, (ranks, width), 1)
    total = None
    for step in range(steps):
        hit = slots_ref[...] - step * width == slot_ids
        one_hot = hit.astype(jnp.float32).astype(jnp.bfloat16)
        parts = jnp.concatenate(split3(shards_ref[step]), axis=0)
        product = lax.dot_general(
            parts, one_hot, (((1,), (1,)), ((), ())), preferred_element_type=jnp.float32
        )
        total = product if total is None else total + product
    joined = join3(total, rows)
    rise_ref[...] = joined[:, : ranks // 2]
    fall_ref[...] = joined[:, ranks // 2 :]


def pick(whole, slots_column, steps):
    _, rows, width = whole.shape
    ranks = slots_column.shape[0]
    half = jax.ShapeDtypeStruct((rows, ranks // 2), jnp.float32)
    return pl.pallas_call(
        pick_kernel,
        grid=(1,),
        in_specs=[
            pl.BlockSpec((ranks, 1), lambda i: (0, 0)),
            pl.BlockSpec((steps, rows, width), lambda i: (0, 0, 0)),
        ],
        out_specs=[pl.BlockSpec((rows, ranks // 2), lambda i: (0, 0))] * 2,
        out_shape=[half, half],
        compiler_params=pltpu.CompilerParams(vmem_limit_bytes=40 * 2**20),
        name="pick",
    )(slots_column, whole)


def place_kernel(crossing_tiles, route_ref, slots_ref, tile_ref, rise_ref, fall_ref, out_ref, parts):
    step = pl.program_id(0)
    rows, width = tile_ref.shape[1:]
    ranks = slots_ref.shape[0]
    tile_id = route_ref[step]

    @pl.when(step == 0)
    def _():
        joined = jnp.concatenate([rise_ref[...], fall_ref[...]], axis=1)
        parts[...] = jnp.concatenate(split3(joined), axis=0)

    @pl.when(tile_id >= crossing_tiles)
    def _():
        out_ref[...] = tile_ref[...]

    @pl.when(tile_id < crossing_tiles)
    def _():
        slot_ids = lax.broadcasted_iota(jnp.int32, (ranks, width), 1) + tile_id * width
        hit = (slots_ref[...] == slot_ids).astype(jnp.float32)
        one_hot = hit.astype(jnp.bfloat16)
        taken = jnp.sum(hit, axis=0, keepdims=True)
        product = jnp.dot(parts[...], one_hot, preferred_element_type=jnp.float32)
        out_ref[0] = jnp.where(taken > 0.0, join3(product, rows), tile_ref[0])


def place(whole, slots_column, climbers, sinkers, route, tile_size, crossing_tiles):
    _, rows, width = whole.shape
    ranks = slots_column.shape[0]
    tile_count = route.shape[0]
    per_shard = width // tile_size
    return pl.pallas_call(
        functools.partial(place_kernel, crossing_tiles),
        grid_spec=pltpu.PrefetchScalarGridSpec(
            num_scalar_prefetch=1,
            grid=(tile_count,),
            in_specs=[
                pl.BlockSpec((ranks, 1), lambda i, r: (0, 0)),
                pl.BlockSpec(
                    (1, rows, tile_size),
                    lambda i, r: (r[i] // per_shard, 0, r[i] % per_shard),
                ),
                pl.BlockSpec((rows, ranks // 2), lambda i, r: (0, 0)),
                pl.BlockSpec((rows, ranks // 2), lambda i, r: (0, 0)),
            ],
            out_specs=pl.BlockSpec((1, rows, tile_size), lambda i, r: (i, 0, 0)),
            scratch_shapes=[pltpu.VMEM((3 * rows, ranks), jnp.bfloat16)],
        ),
        out_shape=jax.ShapeDtypeStruct((tile_count, rows, tile_size), jnp.float32),
        compiler_params=pltpu.CompilerParams(vmem_limit_bytes=40 * 2**20),
        name="place",
    )(route, slots_column, whole, climbers, sinkers)


def pair_kernel(
    share,
    first_ids,
    second_ids,
    live,
    place_ref,
    window_ref,
    tile_ref,
    alive_window_ref,
    alive_tile_ref,
    table_ref,
    table_t_ref,
    out_ref,
    turned,
    first_pos,
    second_pos,
):
    step = pl.program_id(0)
    both = live[first_ids[step]] * live[second_ids[step]]

    @pl.when(both == 0)
    def _():
        out_ref[...] = jnp.zeros_like(out_ref)

    @pl.when(both != 0)
    def _():
        window = window_ref[0]
        rows, lanes = window.shape
        flags = jnp.broadcast_to(alive_window_ref[0], (8, lanes))
        turned[...] = jnp.concatenate([window, flags], axis=0).T
        mine = turned[pl.ds(pl.multiple_of(place_ref[1], share), share), :]
        first_pos[...] = jnp.dot(
            mine[:, :rows], table_t_ref[...], precision=HIGHEST, preferred_element_type=jnp.float32
        )
        second_pos[...] = jnp.dot(
            table_ref[...], tile_ref[0], precision=HIGHEST, preferred_element_type=jnp.float32
        )
        closest = None
        for s in range(SAMPLES):
            gaps = [
                first_pos[:, c * SAMPLES + s : c * SAMPLES + s + 1]
                - second_pos[c * SAMPLES + s : c * SAMPLES + s + 1, :]
                for c in range(3)
            ]
            square = (gaps[0] * gaps[0] + gaps[1] * gaps[1]) + gaps[2] * gaps[2]
            closest = square if closest is None else jnp.minimum(closest, square)
        out_ref[0] = closest * (mine[:, rows : rows + 1] * alive_tile_ref[0])


def pair_blocks(tiles, alive, first_ids, second_ids, row_start, share):
    tile_count, rows, tile_size = tiles.shape
    orders = rows // 3
    table = np.kron(np.eye(3), basis_table(orders)).astype(np.float32)
    live = (jnp.max(alive, axis=1) > 0.0).astype(jnp.int32)
    lanes = min(128, tile_size)
    position = jnp.stack([row_start // lanes, row_start % lanes]).astype(jnp.int32)
    alive = alive.reshape(tile_count, 1, tile_size)
    return pl.pallas_call(
        functools.partial(pair_kernel, share),
        grid_spec=pltpu.PrefetchScalarGridSpec(
            num_scalar_prefetch=4,
            grid=(tile_count,),
            in_specs=[
                pl.BlockSpec((1, rows, lanes), lambda i, a, b, l, w: (a[i], 0, w[0])),
                pl.BlockSpec((1, rows, tile_size), lambda i, a, b, l, w: (b[i], 0, 0)),
                pl.BlockSpec((1, 1, lanes), lambda i, a, b, l, w: (a[i], 0, w[0])),
                pl.BlockSpec((1, 1, tile_size), lambda i, a, b, l, w: (b[i], 0, 0)),
                pl.BlockSpec((3 * SAMPLES, rows), lambda i, a, b, l, w: (0, 0)),
                pl.BlockSpec((rows, 3 * SAMPLES), lambda i, a, b, l, w: (0, 0)),
            ],
            out_specs=pl.BlockSpec((1, share, tile_size), lambda i, a, b, l, w: (i, 0, 0)),
            scratch_shapes=[
                pltpu.VMEM((lanes, rows + 8), jnp.float32),
                pltpu.VMEM((share, 3 * SAMPLES), jnp.float32),
                pltpu.VMEM((3 * SAMPLES, tile_size), jnp.float32),
            ],
        ),
        out_shape=jax.ShapeDtypeStruct((tile_count, share, tile_size), jnp.float32),
        compiler_params=pltpu.CompilerParams(vmem_limit_bytes=40 * 2**20),
        name="pair_blocks",
    )(first_ids, second_ids, live, position, tiles, tiles, alive, alive, table, table.T)


def on_device(chebyshev, crossing, counts, route, pairs):
    orders, _, local = chebyshev.shape
    tm_count = lax.axis_size("tm")
    tile_count = route.shape[1]
    obj_count = local * tm_count
    tile_size = obj_count // tile_count
    share = tile_size // tm_count
    row_start = lax.axis_index("tm") * share

    flat = chebyshev.transpose(1, 0, 2).reshape(3 * orders, local)
    whole = gather(flat, tm_count)

    slot_ids = jnp.arange(tile_size, dtype=jnp.int32)[None, :] + tile_size * route[0][:, None]
    alive_out = (slot_ids < counts[0]).astype(jnp.float32)

    slots_column = crossing[0].reshape(-1, 1)
    rising, falling = pick(whole, slots_column, (tm_count + 1) // 2)
    climbers = shifted(rising, "band", 1)
    sinkers = shifted(falling, "band", -1)
    band_count = lax.axis_size("band")
    core = lax.axis_index("tm") % 2
    halves = route[0].reshape(band_count, 2, tile_count // band_count // 2)
    mine = lax.dynamic_index_in_dim(halves, core, 1, keepdims=False).reshape(-1)
    outgoing = place(whole, slots_column, climbers, sinkers, mine, tile_size, tile_count // 2)
    tiles, alive = exchange(outgoing, alive_out, band_count)
    return pair_blocks(tiles, alive, pairs[0, 0], pairs[0, 1], row_start, share)


def solution(mesh):
    placed = (
        P(None, None, ("band", "tm")),
        P("band", None, None),
        P("band"),
        P("band", None),
        P("band", None, None),
    )
    return jax.shard_map(
        on_device, mesh=mesh, in_specs=placed, out_specs=P("band", "tm", None), check_vma=False
    )
```

```python
import functools

import jax
import jax.numpy as jnp
import numpy as np
from jax import lax
from jax.experimental import pallas as pl
from jax.experimental.pallas import tpu as pltpu
from jax.sharding import PartitionSpec as P

SAMPLES = 64
MESH = pl.DeviceIdType.MESH


def shifted(block, axis, distance):
    devices = range(lax.axis_size(axis))
    route = [(i - distance, i) for i in devices if i - distance in devices]
    return lax.ppermute(block, axis, route)


def basis_table(order_count):
    times = -1.0 + (2.0 * np.arange(SAMPLES) + 1.0) / SAMPLES
    return np.cos(np.arange(order_count)[None, :] * np.arccos(times)[:, None])


def table_parts(order_count):
    rest = basis_table(order_count).astype(np.float32)
    parts = []
    for _ in range(3):
        parts.append(rest.astype(jnp.bfloat16).astype(np.float32))
        rest = rest - parts[-1]
    return parts


def split3(values):
    high = values.astype(jnp.bfloat16)
    rest = values - high.astype(jnp.float32)
    middle = rest.astype(jnp.bfloat16)
    low = (rest - middle.astype(jnp.float32)).astype(jnp.bfloat16)
    return high, middle, low


def join3(product, rows):
    return (product[:rows] + product[rows : 2 * rows]) + product[2 * rows : 3 * rows]


def greet(devices):
    barrier = pltpu.get_barrier_semaphore()
    for device in devices:
        pl.semaphore_signal(barrier, inc=1, device_id=device, device_id_type=MESH)
    pl.semaphore_wait(barrier, len(devices))


def spread(count, position, core, partner, device_of, source_of, out_ref, sems):
    send, recv, hand, take, own = sems
    local = pltpu.make_async_copy(source_of(position), out_ref.at[position, core], own)
    local.start()
    out = []
    for hop in range(1, count):
        peer = (position + hop) % count
        copy = pltpu.make_async_remote_copy(
            src_ref=source_of(peer),
            dst_ref=out_ref.at[position, core],
            send_sem=send.at[hop],
            recv_sem=recv.at[hop],
            device_id=device_of(peer),
            device_id_type=MESH,
        )
        copy.start()
        out.append(copy)
    handed = []
    for hop in range(count):
        origin = (position + count - hop) % count
        if hop:
            out[hop - 1].wait_recv()
        copy = pltpu.make_async_remote_copy(
            src_ref=source_of(position) if hop == 0 else out_ref.at[origin, core],
            dst_ref=out_ref.at[origin, core],
            send_sem=hand.at[hop],
            recv_sem=take.at[hop],
            device_id=partner,
            device_id_type=MESH,
        )
        copy.start()
        handed.append(copy)
    for copy in handed:
        copy.wait()
    for copy in out:
        copy.wait_send()
    local.wait()


def spread_sems(count):
    return [pltpu.SemaphoreType.DMA((count,))] * 4 + [pltpu.SemaphoreType.DMA]


def gather_kernel(count, flat_ref, out_ref, *sems):
    me = lax.axis_index("tm")
    core = me % 2
    partner = {"tm": me + 1 - 2 * core}
    position = me // 2

    def device_of(peer):
        return {"tm": peer * 2 + core}

    greet([device_of((position + hop) % count) for hop in range(1, count)] + [partner])
    spread(count, position, core, partner, device_of, lambda peer: flat_ref, out_ref, sems)


def gather(flat, tm_count):
    count = tm_count // 2
    out = pl.pallas_call(
        functools.partial(gather_kernel, count),
        in_specs=[pl.BlockSpec(memory_space=pl.ANY)],
        out_specs=pl.BlockSpec(memory_space=pl.ANY),
        out_shape=jax.ShapeDtypeStruct((count, 2) + flat.shape, jnp.float32),
        scratch_shapes=spread_sems(count),
        compiler_params=pltpu.CompilerParams(collective_id=0, has_side_effects=True),
        name="gather",
    )(flat)
    return out.reshape((tm_count,) + flat.shape)


def exchange_kernel(count, tiles_ref, flags_ref, out_ref, flags_out_ref, flag_send, flag_recv, flag_own, *sems):
    me = lax.axis_index("tm")
    core = me % 2
    partner = {"tm": me + 1 - 2 * core}
    position = lax.axis_index("band")

    def device_of(peer):
        return {"band": peer}

    greet([device_of((position + hop) % count) for hop in range(1, count)] + [partner])
    own = pltpu.make_async_copy(flags_ref.at[position], flags_out_ref.at[position], flag_own)
    own.start()
    flags = []
    for hop in range(1, count):
        peer = (position + hop) % count
        copy = pltpu.make_async_remote_copy(
            src_ref=flags_ref.at[peer],
            dst_ref=flags_out_ref.at[position],
            send_sem=flag_send.at[hop],
            recv_sem=flag_recv.at[hop],
            device_id=device_of(peer),
            device_id_type=MESH,
        )
        copy.start()
        flags.append(copy)
    spread(
        count, position, core, partner, device_of, lambda peer: tiles_ref.at[peer], out_ref, sems
    )
    for copy in flags:
        copy.wait()
    own.wait()


def exchange(tiles, flags, band_count):
    half, rows, tile_size = tiles.shape
    each = half // band_count
    tiles = tiles.reshape(band_count, each, rows, tile_size)
    flags = flags.reshape(band_count, 2 * each, tile_size)
    out, flags_out = pl.pallas_call(
        functools.partial(exchange_kernel, band_count),
        in_specs=[pl.BlockSpec(memory_space=pl.ANY)] * 2,
        out_specs=[pl.BlockSpec(memory_space=pl.ANY)] * 2,
        out_shape=[
            jax.ShapeDtypeStruct((band_count, 2, each, rows, tile_size), jnp.float32),
            jax.ShapeDtypeStruct(flags.shape, jnp.float32),
        ],
        scratch_shapes=[
            pltpu.SemaphoreType.DMA((band_count,)),
            pltpu.SemaphoreType.DMA((band_count,)),
            pltpu.SemaphoreType.DMA,
        ]
        + spread_sems(band_count),
        compiler_params=pltpu.CompilerParams(collective_id=1, has_side_effects=True),
        name="exchange",
    )(tiles, flags)
    return out.reshape(2 * half, rows, tile_size), flags_out.reshape(2 * half, tile_size)


def pick_kernel(slots_ref, shards_ref, rise_ref, fall_ref):
    steps, rows, width = shards_ref.shape
    ranks = slots_ref.shape[1]
    slot_ids = lax.broadcasted_iota(jnp.int32, (width, ranks), 0)
    total = None
    for step in range(steps):
        hit = slots_ref[...] - step * width == slot_ids
        one_hot = hit.astype(jnp.float32).astype(jnp.bfloat16)
        parts = jnp.concatenate(split3(shards_ref[step]), axis=0)
        product = jnp.dot(parts, one_hot, preferred_element_type=jnp.float32)
        total = product if total is None else total + product
    joined = join3(total, rows)
    rise_ref[...] = joined[:, : ranks // 2]
    fall_ref[...] = joined[:, ranks // 2 :]


def pick(whole, slots_row, steps):
    _, rows, width = whole.shape
    ranks = slots_row.shape[1]
    half = jax.ShapeDtypeStruct((rows, ranks // 2), jnp.float32)
    return pl.pallas_call(
        pick_kernel,
        grid=(1,),
        in_specs=[
            pl.BlockSpec((1, ranks), lambda i: (0, 0)),
            pl.BlockSpec((steps, rows, width), lambda i: (0, 0, 0)),
        ],
        out_specs=[pl.BlockSpec((rows, ranks // 2), lambda i: (0, 0))] * 2,
        out_shape=[half, half],
        compiler_params=pltpu.CompilerParams(vmem_limit_bytes=56 * 2**20),
        name="pick",
    )(slots_row, whole)


def place_kernel(crossing_tiles, route_ref, slots_ref, tile_ref, rise_ref, fall_ref, out_ref, parts):
    step = pl.program_id(0)
    rows, width = tile_ref.shape[1:]
    ranks = slots_ref.shape[1]
    tile_id = route_ref[step]

    @pl.when(step == 0)
    def _():
        joined = jnp.concatenate([rise_ref[...], fall_ref[...]], axis=1)
        ones = jnp.ones((16, ranks), jnp.bfloat16)
        parts[...] = jnp.concatenate(split3(joined) + (ones,), axis=0)

    @pl.when(tile_id >= crossing_tiles)
    def _():
        out_ref[...] = tile_ref[...]

    @pl.when(tile_id < crossing_tiles)
    def _():
        slot_ids = lax.broadcasted_iota(jnp.int32, (width, ranks), 0) + tile_id * width
        one_hot = (slots_ref[...] == slot_ids).astype(jnp.float32).astype(jnp.bfloat16)
        product = lax.dot_general(
            parts[...], one_hot, (((1,), (1,)), ((), ())), preferred_element_type=jnp.float32
        )
        taken = product[3 * rows : 3 * rows + 1]
        merged = join3(product[: 3 * rows], rows)
        out_ref[0] = jnp.where(taken > 0.5, merged, tile_ref[0])


def place(whole, slots_row, climbers, sinkers, route, tile_size, crossing_tiles):
    _, rows, width = whole.shape
    ranks = slots_row.shape[1]
    tile_count = route.shape[0]
    per_shard = width // tile_size
    return pl.pallas_call(
        functools.partial(place_kernel, crossing_tiles),
        grid_spec=pltpu.PrefetchScalarGridSpec(
            num_scalar_prefetch=1,
            grid=(tile_count,),
            in_specs=[
                pl.BlockSpec((1, ranks), lambda i, r: (0, 0)),
                pl.BlockSpec(
                    (1, rows, tile_size),
                    lambda i, r: (r[i] // per_shard, 0, r[i] % per_shard),
                ),
                pl.BlockSpec((rows, ranks // 2), lambda i, r: (0, 0)),
                pl.BlockSpec((rows, ranks // 2), lambda i, r: (0, 0)),
            ],
            out_specs=pl.BlockSpec((1, rows, tile_size), lambda i, r: (i, 0, 0)),
            scratch_shapes=[pltpu.VMEM((3 * rows + 16, ranks), jnp.bfloat16)],
        ),
        out_shape=jax.ShapeDtypeStruct((tile_count, rows, tile_size), jnp.float32),
        compiler_params=pltpu.CompilerParams(vmem_limit_bytes=56 * 2**20),
        name="place",
    )(route, slots_row, whole, climbers, sinkers)


def pair_kernel(
    share,
    first_ids,
    second_ids,
    live,
    place_ref,
    window_ref,
    tile_ref,
    alive_window_ref,
    alive_tile_ref,
    table_ref,
    table_t_ref,
    out_ref,
    turned,
    first_pos,
    second_pos,
):
    step = pl.program_id(0)
    both = live[first_ids[step]] * live[second_ids[step]]

    @pl.when(both == 0)
    def _():
        out_ref[...] = jnp.zeros_like(out_ref)

    @pl.when(both != 0)
    def _():
        window = window_ref[0]
        rows, lanes = window.shape
        flags = jnp.broadcast_to(alive_window_ref[0], (8, lanes))
        turned[...] = jnp.concatenate([window, flags], axis=0).T
        mine = turned[pl.ds(pl.multiple_of(place_ref[1], share), share), :]
        parts = jnp.concatenate(split3(mine[:, :rows]), axis=0)
        product = jnp.dot(parts, table_t_ref[...], preferred_element_type=jnp.float32)
        wide = first_pos.shape[1]

        def term(part, table_part):
            return product[part * share : (part + 1) * share, table_part * wide : (table_part + 1) * wide]

        first_pos[...] = term(0, 0) + (
            (term(0, 1) + term(1, 0)) + ((term(1, 1) + term(0, 2)) + term(2, 0))
        )
        high, middle, low = split3(tile_ref[0])
        orders = rows // 3
        for c in range(3):
            mine_rows = slice(c * orders, (c + 1) * orders)
            packed = [part[mine_rows] for part in (high, middle, high, middle, low, high)]
            second_pos[c * SAMPLES : (c + 1) * SAMPLES, :] = jnp.dot(
                table_ref[...],
                jnp.concatenate(packed, axis=0),
                preferred_element_type=jnp.float32,
            )
        closest = None
        for s in range(SAMPLES):
            gaps = [
                first_pos[:, c * SAMPLES + s : c * SAMPLES + s + 1]
                - second_pos[c * SAMPLES + s : c * SAMPLES + s + 1, :]
                for c in range(3)
            ]
            square = (gaps[0] * gaps[0] + gaps[1] * gaps[1]) + gaps[2] * gaps[2]
            closest = square if closest is None else jnp.minimum(closest, square)
        out_ref[0] = closest * (mine[:, rows : rows + 1] * alive_tile_ref[0])


def pair_blocks(tiles, alive, first_ids, second_ids, row_start, share):
    tile_count, rows, tile_size = tiles.shape
    orders = rows // 3
    wide = 256
    high, middle, low = table_parts(orders)
    table = np.concatenate([high, high, middle, middle, high, low], axis=1)
    spread_parts = [
        np.pad(np.kron(np.eye(3), part.T), ((0, 0), (0, wide - 3 * SAMPLES)))
        for part in (high, middle, low)
    ]
    table_t = np.concatenate(spread_parts, axis=1)
    table, table_t = (jnp.asarray(t, jnp.bfloat16) for t in (table, table_t))
    live = (jnp.max(alive, axis=1) > 0.0).astype(jnp.int32)
    lanes = min(128, tile_size)
    position = jnp.stack([row_start // lanes, row_start % lanes]).astype(jnp.int32)
    alive = alive.reshape(tile_count, 1, tile_size)
    return pl.pallas_call(
        functools.partial(pair_kernel, share),
        grid_spec=pltpu.PrefetchScalarGridSpec(
            num_scalar_prefetch=4,
            grid=(tile_count,),
            in_specs=[
                pl.BlockSpec((1, rows, lanes), lambda i, a, b, l, w: (a[i], 0, w[0])),
                pl.BlockSpec((1, rows, tile_size), lambda i, a, b, l, w: (b[i], 0, 0)),
                pl.BlockSpec((1, 1, lanes), lambda i, a, b, l, w: (a[i], 0, w[0])),
                pl.BlockSpec((1, 1, tile_size), lambda i, a, b, l, w: (b[i], 0, 0)),
                pl.BlockSpec(table.shape, lambda i, a, b, l, w: (0, 0)),
                pl.BlockSpec(table_t.shape, lambda i, a, b, l, w: (0, 0)),
            ],
            out_specs=pl.BlockSpec((1, share, tile_size), lambda i, a, b, l, w: (i, 0, 0)),
            scratch_shapes=[
                pltpu.VMEM((lanes, rows + 8), jnp.float32),
                pltpu.VMEM((share, wide), jnp.float32),
                pltpu.VMEM((3 * SAMPLES, tile_size), jnp.float32),
            ],
        ),
        out_shape=jax.ShapeDtypeStruct((tile_count, share, tile_size), jnp.float32),
        compiler_params=pltpu.CompilerParams(vmem_limit_bytes=56 * 2**20),
        name="pair_blocks",
    )(first_ids, second_ids, live, position, tiles, tiles, alive, alive, table, table_t)


def on_device(chebyshev, crossing, counts, route, pairs):
    orders, _, local = chebyshev.shape
    tm_count = lax.axis_size("tm")
    tile_count = route.shape[1]
    obj_count = local * tm_count
    tile_size = obj_count // tile_count
    share = tile_size // tm_count
    row_start = lax.axis_index("tm") * share

    flat = chebyshev.transpose(1, 0, 2).reshape(3 * orders, local)
    whole = gather(flat, tm_count)

    slot_ids = jnp.arange(tile_size, dtype=jnp.int32)[None, :] + tile_size * route[0][:, None]
    alive_out = (slot_ids < counts[0]).astype(jnp.float32)

    slots_row = crossing[0].reshape(1, -1)
    rising, falling = pick(whole, slots_row, (tm_count + 1) // 2)
    climbers = shifted(rising, "band", 1)
    sinkers = shifted(falling, "band", -1)
    band_count = lax.axis_size("band")
    core = lax.axis_index("tm") % 2
    halves = route[0].reshape(band_count, 2, tile_count // band_count // 2)
    mine = lax.dynamic_index_in_dim(halves, core, 1, keepdims=False).reshape(-1)
    outgoing = place(whole, slots_row, climbers, sinkers, mine, tile_size, tile_count // 2)
    tiles, alive = exchange(outgoing, alive_out, band_count)
    return pair_blocks(tiles, alive, pairs[0, 0], pairs[0, 1], row_start, share)


def solution(mesh):
    placed = (
        P(None, None, ("band", "tm")),
        P("band", None, None),
        P("band"),
        P("band", None),
        P("band", None, None),
    )
    return jax.shard_map(
        on_device, mesh=mesh, in_specs=placed, out_specs=P("band", "tm", None), check_vma=False
    )
```

```python
import functools

import jax
import jax.numpy as jnp
import numpy as np
from jax import lax
from jax.experimental import pallas as pl
from jax.experimental.pallas import tpu as pltpu
from jax.sharding import PartitionSpec as P

SAMPLES = 64
MESH = pl.DeviceIdType.MESH


def shifted(block, axis, distance):
    devices = range(lax.axis_size(axis))
    route = [(i - distance, i) for i in devices if i - distance in devices]
    return lax.ppermute(block, axis, route)


def basis_table(order_count):
    times = -1.0 + (2.0 * np.arange(SAMPLES) + 1.0) / SAMPLES
    return np.cos(np.arange(order_count)[None, :] * np.arccos(times)[:, None])


def table_parts(order_count):
    rest = basis_table(order_count).astype(np.float32)
    parts = []
    for _ in range(3):
        parts.append(rest.astype(jnp.bfloat16).astype(np.float32))
        rest = rest - parts[-1]
    return parts


def split3(values):
    high = values.astype(jnp.bfloat16)
    rest = values - high.astype(jnp.float32)
    middle = rest.astype(jnp.bfloat16)
    low = (rest - middle.astype(jnp.float32)).astype(jnp.bfloat16)
    return high, middle, low


def join3(product, rows):
    return (product[:rows] + product[rows : 2 * rows]) + product[2 * rows : 3 * rows]


def greet(devices):
    barrier = pltpu.get_barrier_semaphore()
    for device in devices:
        pl.semaphore_signal(barrier, inc=1, device_id=device, device_id_type=MESH)
    pl.semaphore_wait(barrier, len(devices))


def spread(count, position, core, partner, device_of, source_of, out_ref, sems):
    send, recv, hand, take, own = sems
    local = pltpu.make_async_copy(source_of(position), out_ref.at[position, core], own)
    local.start()
    out = []
    for hop in range(1, count):
        peer = (position + hop) % count
        copy = pltpu.make_async_remote_copy(
            src_ref=source_of(peer),
            dst_ref=out_ref.at[position, core],
            send_sem=send.at[hop],
            recv_sem=recv.at[hop],
            device_id=device_of(peer),
            device_id_type=MESH,
        )
        copy.start()
        out.append(copy)
    handed = []
    for hop in range(count):
        origin = (position + count - hop) % count
        if hop:
            out[hop - 1].wait_recv()
        copy = pltpu.make_async_remote_copy(
            src_ref=source_of(position) if hop == 0 else out_ref.at[origin, core],
            dst_ref=out_ref.at[origin, core],
            send_sem=hand.at[hop],
            recv_sem=take.at[hop],
            device_id=partner,
            device_id_type=MESH,
        )
        copy.start()
        handed.append(copy)
    for copy in handed:
        copy.wait()
    for copy in out:
        copy.wait_send()
    local.wait()


def spread_sems(count):
    return [pltpu.SemaphoreType.DMA((count,))] * 4 + [pltpu.SemaphoreType.DMA]


def gather_kernel(count, flat_ref, out_ref, *sems):
    me = lax.axis_index("tm")
    core = me % 2
    partner = {"tm": me + 1 - 2 * core}
    position = me // 2

    def device_of(peer):
        return {"tm": peer * 2 + core}

    greet([device_of((position + hop) % count) for hop in range(1, count)] + [partner])
    spread(count, position, core, partner, device_of, lambda peer: flat_ref, out_ref, sems)


def gather(flat, tm_count):
    count = tm_count // 2
    out = pl.pallas_call(
        functools.partial(gather_kernel, count),
        in_specs=[pl.BlockSpec(memory_space=pl.ANY)],
        out_specs=pl.BlockSpec(memory_space=pl.ANY),
        out_shape=jax.ShapeDtypeStruct((count, 2) + flat.shape, jnp.float32),
        scratch_shapes=spread_sems(count),
        compiler_params=pltpu.CompilerParams(collective_id=0, has_side_effects=True),
        name="gather",
    )(flat)
    return out.reshape((tm_count,) + flat.shape)


def exchange_kernel(count, tiles_ref, flags_ref, out_ref, flags_out_ref, flag_send, flag_recv, flag_own, *sems):
    me = lax.axis_index("tm")
    core = me % 2
    partner = {"tm": me + 1 - 2 * core}
    position = lax.axis_index("band")

    def device_of(peer):
        return {"band": peer}

    greet([device_of((position + hop) % count) for hop in range(1, count)] + [partner])
    own = pltpu.make_async_copy(flags_ref.at[position], flags_out_ref.at[position], flag_own)
    own.start()
    flags = []
    for hop in range(1, count):
        peer = (position + hop) % count
        copy = pltpu.make_async_remote_copy(
            src_ref=flags_ref.at[peer],
            dst_ref=flags_out_ref.at[position],
            send_sem=flag_send.at[hop],
            recv_sem=flag_recv.at[hop],
            device_id=device_of(peer),
            device_id_type=MESH,
        )
        copy.start()
        flags.append(copy)
    spread(
        count, position, core, partner, device_of, lambda peer: tiles_ref.at[peer], out_ref, sems
    )
    for copy in flags:
        copy.wait()
    own.wait()


def exchange(tiles, flags, band_count):
    half, rows, tile_size = tiles.shape
    each = half // band_count
    tiles = tiles.reshape(band_count, each, rows, tile_size)
    flags = flags.reshape(band_count, 2 * each, tile_size)
    out, flags_out = pl.pallas_call(
        functools.partial(exchange_kernel, band_count),
        in_specs=[pl.BlockSpec(memory_space=pl.ANY)] * 2,
        out_specs=[pl.BlockSpec(memory_space=pl.ANY)] * 2,
        out_shape=[
            jax.ShapeDtypeStruct((band_count, 2, each, rows, tile_size), jnp.float32),
            jax.ShapeDtypeStruct(flags.shape, jnp.float32),
        ],
        scratch_shapes=[
            pltpu.SemaphoreType.DMA((band_count,)),
            pltpu.SemaphoreType.DMA((band_count,)),
            pltpu.SemaphoreType.DMA,
        ]
        + spread_sems(band_count),
        compiler_params=pltpu.CompilerParams(collective_id=1, has_side_effects=True),
        name="exchange",
    )(tiles, flags)
    return out.reshape(2 * half, rows, tile_size), flags_out.reshape(2 * half, tile_size)


def pick_kernel(slots_ref, shards_ref, rise_ref, fall_ref):
    steps, rows, width = shards_ref.shape
    ranks = slots_ref.shape[1]
    slot_ids = lax.broadcasted_iota(jnp.int32, (width, ranks), 0)
    total = None
    for step in range(steps):
        hit = slots_ref[...] - step * width == slot_ids
        one_hot = hit.astype(jnp.float32).astype(jnp.bfloat16)
        parts = jnp.concatenate(split3(shards_ref[step]), axis=0)
        product = jnp.dot(parts, one_hot, preferred_element_type=jnp.float32)
        total = product if total is None else total + product
    joined = join3(total, rows)
    rise_ref[...] = joined[:, : ranks // 2]
    fall_ref[...] = joined[:, ranks // 2 :]


def pick(whole, slots_row, steps):
    _, rows, width = whole.shape
    ranks = slots_row.shape[1]
    half = jax.ShapeDtypeStruct((rows, ranks // 2), jnp.float32)
    return pl.pallas_call(
        pick_kernel,
        grid=(1,),
        in_specs=[
            pl.BlockSpec((1, ranks), lambda i: (0, 0)),
            pl.BlockSpec((steps, rows, width), lambda i: (0, 0, 0)),
        ],
        out_specs=[pl.BlockSpec((rows, ranks // 2), lambda i: (0, 0))] * 2,
        out_shape=[half, half],
        compiler_params=pltpu.CompilerParams(vmem_limit_bytes=40 * 2**20),
        name="pick",
    )(slots_row, whole)


def place_kernel(crossing_tiles, route_ref, slots_ref, tile_ref, rise_ref, fall_ref, out_ref, parts):
    step = pl.program_id(0)
    rows, width = tile_ref.shape[1:]
    ranks = slots_ref.shape[0]
    tile_id = route_ref[step]

    @pl.when(step == 0)
    def _():
        joined = jnp.concatenate([rise_ref[...], fall_ref[...]], axis=1)
        parts[...] = jnp.concatenate(split3(joined), axis=0)

    @pl.when(tile_id >= crossing_tiles)
    def _():
        out_ref[...] = tile_ref[...]

    @pl.when(tile_id < crossing_tiles)
    def _():
        slot_ids = lax.broadcasted_iota(jnp.int32, (ranks, width), 1) + tile_id * width
        hit = (slots_ref[...] == slot_ids).astype(jnp.float32)
        one_hot = hit.astype(jnp.bfloat16)
        taken = jnp.sum(hit, axis=0, keepdims=True)
        product = jnp.dot(parts[...], one_hot, preferred_element_type=jnp.float32)
        out_ref[0] = jnp.where(taken > 0.0, join3(product, rows), tile_ref[0])


def place(whole, slots_column, climbers, sinkers, route, tile_size, crossing_tiles):
    _, rows, width = whole.shape
    ranks = slots_column.shape[0]
    tile_count = route.shape[0]
    per_shard = width // tile_size
    return pl.pallas_call(
        functools.partial(place_kernel, crossing_tiles),
        grid_spec=pltpu.PrefetchScalarGridSpec(
            num_scalar_prefetch=1,
            grid=(tile_count,),
            in_specs=[
                pl.BlockSpec((ranks, 1), lambda i, r: (0, 0)),
                pl.BlockSpec(
                    (1, rows, tile_size),
                    lambda i, r: (r[i] // per_shard, 0, r[i] % per_shard),
                ),
                pl.BlockSpec((rows, ranks // 2), lambda i, r: (0, 0)),
                pl.BlockSpec((rows, ranks // 2), lambda i, r: (0, 0)),
            ],
            out_specs=pl.BlockSpec((1, rows, tile_size), lambda i, r: (i, 0, 0)),
            scratch_shapes=[pltpu.VMEM((3 * rows, ranks), jnp.bfloat16)],
        ),
        out_shape=jax.ShapeDtypeStruct((tile_count, rows, tile_size), jnp.float32),
        compiler_params=pltpu.CompilerParams(vmem_limit_bytes=40 * 2**20),
        name="place",
    )(route, slots_column, whole, climbers, sinkers)


def pair_kernel(
    share,
    first_ids,
    second_ids,
    live,
    place_ref,
    tiles_ref,
    alive_ref,
    table_ref,
    table_t_ref,
    out_ref,
    turned,
    first_pos,
    second_pos,
):
    step = pl.program_id(0)
    first_id = first_ids[step]
    second_id = second_ids[step]
    lanes = turned.shape[0]
    both = live[first_id] * live[second_id]

    @pl.when(both == 0)
    def _():
        out_ref[...] = jnp.zeros_like(out_ref)

    @pl.when(both != 0)
    def _():
        columns = pl.ds(pl.multiple_of(place_ref[0] * lanes, lanes), lanes)
        window = tiles_ref[first_id, :, columns]
        rows = window.shape[0]
        flags = jnp.broadcast_to(alive_ref[first_id, :, columns], (8, lanes))
        turned[...] = jnp.concatenate([window, flags], axis=0).T
        mine = turned[pl.ds(pl.multiple_of(place_ref[1], share), share), :]
        parts = jnp.concatenate(split3(mine[:, :rows]), axis=0)
        product = jnp.dot(parts, table_t_ref[...], preferred_element_type=jnp.float32)
        wide = first_pos.shape[1]

        def term(part, table_part):
            return product[part * share : (part + 1) * share, table_part * wide : (table_part + 1) * wide]

        first_pos[...] = term(0, 0) + (
            (term(0, 1) + term(1, 0)) + ((term(1, 1) + term(0, 2)) + term(2, 0))
        )
        high, middle, low = split3(tiles_ref[second_id])
        orders = rows // 3
        for c in range(3):
            mine_rows = slice(c * orders, (c + 1) * orders)
            packed = [part[mine_rows] for part in (high, middle, high, middle, low, high)]
            second_pos[c * SAMPLES : (c + 1) * SAMPLES, :] = jnp.dot(
                table_ref[...],
                jnp.concatenate(packed, axis=0),
                preferred_element_type=jnp.float32,
            )
        closest = None
        for s in range(SAMPLES):
            gaps = [
                first_pos[:, c * SAMPLES + s : c * SAMPLES + s + 1]
                - second_pos[c * SAMPLES + s : c * SAMPLES + s + 1, :]
                for c in range(3)
            ]
            square = (gaps[0] * gaps[0] + gaps[1] * gaps[1]) + gaps[2] * gaps[2]
            closest = square if closest is None else jnp.minimum(closest, square)
        out_ref[0] = closest * (mine[:, rows : rows + 1] * alive_ref[second_id])


def pair_blocks(tiles, alive, first_ids, second_ids, row_start, share):
    tile_count, rows, tile_size = tiles.shape
    orders = rows // 3
    wide = 256
    high, middle, low = table_parts(orders)
    table = np.concatenate([high, high, middle, middle, high, low], axis=1)
    spread_parts = [
        np.pad(np.kron(np.eye(3), part.T), ((0, 0), (0, wide - 3 * SAMPLES)))
        for part in (high, middle, low)
    ]
    table_t = np.concatenate(spread_parts, axis=1)
    table, table_t = (jnp.asarray(t, jnp.bfloat16) for t in (table, table_t))
    live = (jnp.max(alive, axis=1) > 0.0).astype(jnp.int32)
    lanes = min(128, tile_size)
    position = jnp.stack([row_start // lanes, row_start % lanes]).astype(jnp.int32)
    alive = alive.reshape(tile_count, 1, tile_size)
    return pl.pallas_call(
        functools.partial(pair_kernel, share),
        grid_spec=pltpu.PrefetchScalarGridSpec(
            num_scalar_prefetch=4,
            grid=(tile_count,),
            in_specs=[
                pl.BlockSpec(tiles.shape, lambda i, a, b, l, w: (0, 0, 0)),
                pl.BlockSpec(alive.shape, lambda i, a, b, l, w: (0, 0, 0)),
                pl.BlockSpec(table.shape, lambda i, a, b, l, w: (0, 0)),
                pl.BlockSpec(table_t.shape, lambda i, a, b, l, w: (0, 0)),
            ],
            out_specs=pl.BlockSpec((1, share, tile_size), lambda i, a, b, l, w: (i, 0, 0)),
            scratch_shapes=[
                pltpu.VMEM((lanes, rows + 8), jnp.float32),
                pltpu.VMEM((share, wide), jnp.float32),
                pltpu.VMEM((3 * SAMPLES, tile_size), jnp.float32),
            ],
        ),
        out_shape=jax.ShapeDtypeStruct((tile_count, share, tile_size), jnp.float32),
        compiler_params=pltpu.CompilerParams(vmem_limit_bytes=40 * 2**20),
        name="pair_blocks",
    )(first_ids, second_ids, live, position, tiles, alive, table, table_t)


def on_device(chebyshev, crossing, counts, route, pairs):
    orders, _, local = chebyshev.shape
    tm_count = lax.axis_size("tm")
    tile_count = route.shape[1]
    obj_count = local * tm_count
    tile_size = obj_count // tile_count
    share = tile_size // tm_count
    row_start = lax.axis_index("tm") * share

    flat = chebyshev.transpose(1, 0, 2).reshape(3 * orders, local)
    whole = gather(flat, tm_count)

    slot_ids = jnp.arange(tile_size, dtype=jnp.int32)[None, :] + tile_size * route[0][:, None]
    alive_out = (slot_ids < counts[0]).astype(jnp.float32)

    slots_row = crossing[0].reshape(1, -1)
    rising, falling = pick(whole, slots_row, (tm_count + 1) // 2)
    climbers = shifted(rising, "band", 1)
    sinkers = shifted(falling, "band", -1)
    band_count = lax.axis_size("band")
    core = lax.axis_index("tm") % 2
    halves = route[0].reshape(band_count, 2, tile_count // band_count // 2)
    mine = lax.dynamic_index_in_dim(halves, core, 1, keepdims=False).reshape(-1)
    slots_column = crossing[0].reshape(-1, 1)
    outgoing = place(whole, slots_column, climbers, sinkers, mine, tile_size, tile_count // 2)
    tiles, alive = exchange(outgoing, alive_out, band_count)
    return pair_blocks(tiles, alive, pairs[0, 0], pairs[0, 1], row_start, share)


def solution(mesh):
    placed = (
        P(None, None, ("band", "tm")),
        P("band", None, None),
        P("band"),
        P("band", None),
        P("band", None, None),
    )
    return jax.shard_map(
        on_device, mesh=mesh, in_specs=placed, out_specs=P("band", "tm", None), check_vma=False
    )
```

```python
import functools

import jax
import jax.numpy as jnp
import numpy as np
from jax import lax
from jax.experimental import pallas as pl
from jax.experimental.pallas import tpu as pltpu
from jax.sharding import PartitionSpec as P

SAMPLES = 64
MESH = pl.DeviceIdType.MESH


def shifted(block, axis, distance):
    devices = range(lax.axis_size(axis))
    route = [(i - distance, i) for i in devices if i - distance in devices]
    return lax.ppermute(block, axis, route)


def basis_table(order_count):
    times = -1.0 + (2.0 * np.arange(SAMPLES) + 1.0) / SAMPLES
    return np.cos(np.arange(order_count)[None, :] * np.arccos(times)[:, None])


def table_parts(order_count):
    rest = basis_table(order_count).astype(np.float32)
    parts = []
    for _ in range(3):
        parts.append(rest.astype(jnp.bfloat16).astype(np.float32))
        rest = rest - parts[-1]
    return parts


def split3(values):
    high = values.astype(jnp.bfloat16)
    rest = values - high.astype(jnp.float32)
    middle = rest.astype(jnp.bfloat16)
    low = (rest - middle.astype(jnp.float32)).astype(jnp.bfloat16)
    return high, middle, low


def join3(product, rows):
    return (product[:rows] + product[rows : 2 * rows]) + product[2 * rows : 3 * rows]


def greet(devices):
    barrier = pltpu.get_barrier_semaphore()
    for device in devices:
        pl.semaphore_signal(barrier, inc=1, device_id=device, device_id_type=MESH)
    pl.semaphore_wait(barrier, len(devices))


def spread(count, pieces, position, core, partner, device_of, source_of, out_ref, sems):
    send, recv, hand, take, own = sems
    local = pltpu.make_async_copy(source_of(position), out_ref.at[position, core], own)
    local.start()
    size = out_ref.shape[2] // pieces
    out = {}
    for piece in range(pieces):
        cut = pl.ds(piece * size, size)
        for hop in range(1, count):
            peer = (position + hop) % count
            copy = pltpu.make_async_remote_copy(
                src_ref=source_of(peer).at[cut],
                dst_ref=out_ref.at[position, core, cut],
                send_sem=send.at[piece * count + hop],
                recv_sem=recv.at[piece * count + hop],
                device_id=device_of(peer),
                device_id_type=MESH,
            )
            copy.start()
            out[piece, hop] = copy
    handed = []
    for piece in range(pieces):
        cut = pl.ds(piece * size, size)
        for hop in range(count):
            origin = (position + count - hop) % count
            if hop:
                out[piece, hop].wait_recv()
                source = out_ref.at[origin, core, cut]
            else:
                source = source_of(position).at[cut]
            copy = pltpu.make_async_remote_copy(
                src_ref=source,
                dst_ref=out_ref.at[origin, core, cut],
                send_sem=hand.at[piece * count + hop],
                recv_sem=take.at[piece * count + hop],
                device_id=partner,
                device_id_type=MESH,
            )
            copy.start()
            handed.append(copy)
    for copy in handed:
        copy.wait()
    for copy in out.values():
        copy.wait_send()
    local.wait()


def spread_sems(count, pieces):
    return [pltpu.SemaphoreType.DMA((count * pieces,))] * 4 + [pltpu.SemaphoreType.DMA]


def gather_kernel(count, flat_ref, out_ref, *sems):
    me = lax.axis_index("tm")
    core = me % 2
    partner = {"tm": me + 1 - 2 * core}
    position = me // 2

    def device_of(peer):
        return {"tm": peer * 2 + core}

    greet([device_of((position + hop) % count) for hop in range(1, count)] + [partner])
    spread(count, 4, position, core, partner, device_of, lambda peer: flat_ref, out_ref, sems)


def gather(flat, tm_count):
    count = tm_count // 2
    out = pl.pallas_call(
        functools.partial(gather_kernel, count),
        in_specs=[pl.BlockSpec(memory_space=pl.ANY)],
        out_specs=pl.BlockSpec(memory_space=pl.ANY),
        out_shape=jax.ShapeDtypeStruct((count, 2) + flat.shape, jnp.float32),
        scratch_shapes=spread_sems(count, 4),
        compiler_params=pltpu.CompilerParams(collective_id=0, has_side_effects=True),
        name="gather",
    )(flat)
    return out.reshape((tm_count,) + flat.shape)


def exchange_kernel(count, tiles_ref, flags_ref, out_ref, flags_out_ref, flag_send, flag_recv, flag_own, *sems):
    me = lax.axis_index("tm")
    core = me % 2
    partner = {"tm": me + 1 - 2 * core}
    position = lax.axis_index("band")

    def device_of(peer):
        return {"band": peer}

    greet([device_of((position + hop) % count) for hop in range(1, count)] + [partner])
    own = pltpu.make_async_copy(flags_ref.at[position], flags_out_ref.at[position], flag_own)
    own.start()
    flags = []
    for hop in range(1, count):
        peer = (position + hop) % count
        copy = pltpu.make_async_remote_copy(
            src_ref=flags_ref.at[peer],
            dst_ref=flags_out_ref.at[position],
            send_sem=flag_send.at[hop],
            recv_sem=flag_recv.at[hop],
            device_id=device_of(peer),
            device_id_type=MESH,
        )
        copy.start()
        flags.append(copy)
    spread(
        count,
        min(2, out_ref.shape[2]),
        position,
        core,
        partner,
        device_of,
        lambda peer: tiles_ref.at[peer],
        out_ref,
        sems,
    )
    for copy in flags:
        copy.wait()
    own.wait()


def exchange(tiles, flags, band_count):
    half, rows, tile_size = tiles.shape
    each = half // band_count
    tiles = tiles.reshape(band_count, each, rows, tile_size)
    flags = flags.reshape(band_count, 2 * each, tile_size)
    out, flags_out = pl.pallas_call(
        functools.partial(exchange_kernel, band_count),
        in_specs=[pl.BlockSpec(memory_space=pl.ANY)] * 2,
        out_specs=[pl.BlockSpec(memory_space=pl.ANY)] * 2,
        out_shape=[
            jax.ShapeDtypeStruct((band_count, 2, each, rows, tile_size), jnp.float32),
            jax.ShapeDtypeStruct(flags.shape, jnp.float32),
        ],
        scratch_shapes=[
            pltpu.SemaphoreType.DMA((band_count,)),
            pltpu.SemaphoreType.DMA((band_count,)),
            pltpu.SemaphoreType.DMA,
        ]
        + spread_sems(band_count, min(2, each)),
        compiler_params=pltpu.CompilerParams(collective_id=1, has_side_effects=True),
        name="exchange",
    )(tiles, flags)
    return out.reshape(2 * half, rows, tile_size), flags_out.reshape(2 * half, tile_size)


def pick_kernel(slots_ref, shards_ref, rise_ref, fall_ref):
    steps, rows, width = shards_ref.shape
    ranks = slots_ref.shape[1]
    slot_ids = lax.broadcasted_iota(jnp.int32, (width, ranks), 0)
    total = None
    for step in range(steps):
        hit = slots_ref[...] - step * width == slot_ids
        one_hot = hit.astype(jnp.float32).astype(jnp.bfloat16)
        parts = jnp.concatenate(split3(shards_ref[step]), axis=0)
        product = jnp.dot(parts, one_hot, preferred_element_type=jnp.float32)
        total = product if total is None else total + product
    joined = join3(total, rows)
    rise_ref[...] = joined[:, : ranks // 2]
    fall_ref[...] = joined[:, ranks // 2 :]


def pick(whole, slots_row, steps):
    _, rows, width = whole.shape
    ranks = slots_row.shape[1]
    half = jax.ShapeDtypeStruct((rows, ranks // 2), jnp.float32)
    return pl.pallas_call(
        pick_kernel,
        grid=(1,),
        in_specs=[
            pl.BlockSpec((1, ranks), lambda i: (0, 0)),
            pl.BlockSpec((steps, rows, width), lambda i: (0, 0, 0)),
        ],
        out_specs=[pl.BlockSpec((rows, ranks // 2), lambda i: (0, 0))] * 2,
        out_shape=[half, half],
        compiler_params=pltpu.CompilerParams(vmem_limit_bytes=40 * 2**20),
        name="pick",
    )(slots_row, whole)


def place_kernel(crossing_tiles, route_ref, slots_ref, tile_ref, rise_ref, fall_ref, out_ref, parts):
    step = pl.program_id(0)
    rows, width = tile_ref.shape[1:]
    ranks = slots_ref.shape[0]
    tile_id = route_ref[step]

    @pl.when(step == 0)
    def _():
        joined = jnp.concatenate([rise_ref[...], fall_ref[...]], axis=1)
        parts[...] = jnp.concatenate(split3(joined), axis=0)

    @pl.when(tile_id >= crossing_tiles)
    def _():
        out_ref[...] = tile_ref[...]

    @pl.when(tile_id < crossing_tiles)
    def _():
        slot_ids = lax.broadcasted_iota(jnp.int32, (ranks, width), 1) + tile_id * width
        hit = (slots_ref[...] == slot_ids).astype(jnp.float32)
        one_hot = hit.astype(jnp.bfloat16)
        taken = jnp.sum(hit, axis=0, keepdims=True)
        product = jnp.dot(parts[...], one_hot, preferred_element_type=jnp.float32)
        out_ref[0] = jnp.where(taken > 0.0, join3(product, rows), tile_ref[0])


def place(whole, slots_column, climbers, sinkers, route, tile_size, crossing_tiles):
    _, rows, width = whole.shape
    ranks = slots_column.shape[0]
    tile_count = route.shape[0]
    per_shard = width // tile_size
    return pl.pallas_call(
        functools.partial(place_kernel, crossing_tiles),
        grid_spec=pltpu.PrefetchScalarGridSpec(
            num_scalar_prefetch=1,
            grid=(tile_count,),
            in_specs=[
                pl.BlockSpec((ranks, 1), lambda i, r: (0, 0)),
                pl.BlockSpec(
                    (1, rows, tile_size),
                    lambda i, r: (r[i] // per_shard, 0, r[i] % per_shard),
                ),
                pl.BlockSpec((rows, ranks // 2), lambda i, r: (0, 0)),
                pl.BlockSpec((rows, ranks // 2), lambda i, r: (0, 0)),
            ],
            out_specs=pl.BlockSpec((1, rows, tile_size), lambda i, r: (i, 0, 0)),
            scratch_shapes=[pltpu.VMEM((3 * rows, ranks), jnp.bfloat16)],
        ),
        out_shape=jax.ShapeDtypeStruct((tile_count, rows, tile_size), jnp.float32),
        compiler_params=pltpu.CompilerParams(vmem_limit_bytes=40 * 2**20),
        name="place",
    )(route, slots_column, whole, climbers, sinkers)


def pair_kernel(
    share,
    first_ids,
    second_ids,
    live,
    place_ref,
    tiles_ref,
    alive_ref,
    table_ref,
    table_t_ref,
    out_ref,
    turned,
    first_pos,
    second_pos,
):
    step = pl.program_id(0)
    first_id = first_ids[step]
    second_id = second_ids[step]
    lanes = turned.shape[0]
    both = live[first_id] * live[second_id]

    @pl.when(both == 0)
    def _():
        out_ref[...] = jnp.zeros_like(out_ref)

    @pl.when(both != 0)
    def _():
        columns = pl.ds(pl.multiple_of(place_ref[0] * lanes, lanes), lanes)
        window = tiles_ref[first_id, :, columns]
        rows = window.shape[0]
        flags = jnp.broadcast_to(alive_ref[first_id, :, columns], (8, lanes))
        turned[...] = jnp.concatenate([window, flags], axis=0).T
        mine = turned[pl.ds(pl.multiple_of(place_ref[1], share), share), :]
        parts = jnp.concatenate(split3(mine[:, :rows]), axis=0)
        product = jnp.dot(parts, table_t_ref[...], preferred_element_type=jnp.float32)
        wide = first_pos.shape[1]

        def term(part, table_part):
            return product[part * share : (part + 1) * share, table_part * wide : (table_part + 1) * wide]

        first_pos[...] = term(0, 0) + (
            (term(0, 1) + term(1, 0)) + ((term(1, 1) + term(0, 2)) + term(2, 0))
        )
        high, middle, low = split3(tiles_ref[second_id])
        orders = rows // 3
        for c in range(3):
            mine_rows = slice(c * orders, (c + 1) * orders)
            packed = [part[mine_rows] for part in (high, middle, high, middle, low, high)]
            second_pos[c * SAMPLES : (c + 1) * SAMPLES, :] = jnp.dot(
                table_ref[...],
                jnp.concatenate(packed, axis=0),
                preferred_element_type=jnp.float32,
            )
        closest = None
        for s in range(SAMPLES):
            gaps = [
                first_pos[:, c * SAMPLES + s : c * SAMPLES + s + 1]
                - second_pos[c * SAMPLES + s : c * SAMPLES + s + 1, :]
                for c in range(3)
            ]
            square = (gaps[0] * gaps[0] + gaps[1] * gaps[1]) + gaps[2] * gaps[2]
            closest = square if closest is None else jnp.minimum(closest, square)
        out_ref[0] = closest * (mine[:, rows : rows + 1] * alive_ref[second_id])


def pair_blocks(tiles, alive, first_ids, second_ids, row_start, share):
    tile_count, rows, tile_size = tiles.shape
    orders = rows // 3
    wide = 256
    high, middle, low = table_parts(orders)
    table = np.concatenate([high, high, middle, middle, high, low], axis=1)
    spread_parts = [
        np.pad(np.kron(np.eye(3), part.T), ((0, 0), (0, wide - 3 * SAMPLES)))
        for part in (high, middle, low)
    ]
    table_t = np.concatenate(spread_parts, axis=1)
    table, table_t = (jnp.asarray(t, jnp.bfloat16) for t in (table, table_t))
    live = (jnp.max(alive, axis=1) > 0.0).astype(jnp.int32)
    lanes = min(128, tile_size)
    position = jnp.stack([row_start // lanes, row_start % lanes]).astype(jnp.int32)
    alive = alive.reshape(tile_count, 1, tile_size)
    return pl.pallas_call(
        functools.partial(pair_kernel, share),
        grid_spec=pltpu.PrefetchScalarGridSpec(
            num_scalar_prefetch=4,
            grid=(tile_count,),
            in_specs=[
                pl.BlockSpec(tiles.shape, lambda i, a, b, l, w: (0, 0, 0)),
                pl.BlockSpec(alive.shape, lambda i, a, b, l, w: (0, 0, 0)),
                pl.BlockSpec(table.shape, lambda i, a, b, l, w: (0, 0)),
                pl.BlockSpec(table_t.shape, lambda i, a, b, l, w: (0, 0)),
            ],
            out_specs=pl.BlockSpec((1, share, tile_size), lambda i, a, b, l, w: (i, 0, 0)),
            scratch_shapes=[
                pltpu.VMEM((lanes, rows + 8), jnp.float32),
                pltpu.VMEM((share, wide), jnp.float32),
                pltpu.VMEM((3 * SAMPLES, tile_size), jnp.float32),
            ],
        ),
        out_shape=jax.ShapeDtypeStruct((tile_count, share, tile_size), jnp.float32),
        compiler_params=pltpu.CompilerParams(vmem_limit_bytes=40 * 2**20),
        name="pair_blocks",
    )(first_ids, second_ids, live, position, tiles, alive, table, table_t)


def on_device(chebyshev, crossing, counts, route, pairs):
    orders, _, local = chebyshev.shape
    tm_count = lax.axis_size("tm")
    tile_count = route.shape[1]
    obj_count = local * tm_count
    tile_size = obj_count // tile_count
    share = tile_size // tm_count
    row_start = lax.axis_index("tm") * share

    flat = chebyshev.transpose(1, 0, 2).reshape(3 * orders, local)
    whole = gather(flat, tm_count)

    slot_ids = jnp.arange(tile_size, dtype=jnp.int32)[None, :] + tile_size * route[0][:, None]
    alive_out = (slot_ids < counts[0]).astype(jnp.float32)

    slots_row = crossing[0].reshape(1, -1)
    rising, falling = pick(whole, slots_row, (tm_count + 1) // 2)
    climbers = shifted(rising, "band", 1)
    sinkers = shifted(falling, "band", -1)
    band_count = lax.axis_size("band")
    core = lax.axis_index("tm") % 2
    halves = route[0].reshape(band_count, 2, tile_count // band_count // 2)
    mine = lax.dynamic_index_in_dim(halves, core, 1, keepdims=False).reshape(-1)
    slots_column = crossing[0].reshape(-1, 1)
    outgoing = place(whole, slots_column, climbers, sinkers, mine, tile_size, tile_count // 2)
    tiles, alive = exchange(outgoing, alive_out, band_count)
    return pair_blocks(tiles, alive, pairs[0, 0], pairs[0, 1], row_start, share)


def solution(mesh):
    placed = (
        P(None, None, ("band", "tm")),
        P("band", None, None),
        P("band"),
        P("band", None),
        P("band", None, None),
    )
    return jax.shard_map(
        on_device, mesh=mesh, in_specs=placed, out_specs=P("band", "tm", None), check_vma=False
    )
```
